256 devices in a mesh: grp: 8 (over x, y_hi), blk: 32 (over y_lo, z, core).
Axes of the slice: x: 4, y: 4 (y_hi: 2, y_lo: 2; y = y_hi * 2 + y_lo), z: 8, core: 2. Of those that a mesh axis runs over, the one named last changes fastest.
Arguments:
- amplitudes: float32 [8192, 1176], P(('grp', 'blk')), may hold values from -6 to 6
- integrals: float32 [8192, 65536], P(('grp', 'blk')), may hold values from -0.0625 to 0.0625
Outputs:
- ladder: float32 [1176, 65536], P('grp', 'blk')
The draws below stay inside these ranges and needn't reach their ends.
All inputs are finite; a program needn't handle non-finite values.
Results may differ from the reference program's by a relative error of at most 0.00007.
Values sent between devices are 32-bit elements; how exact they have to be, the bound alone decides.
No kernel may reach another device: no remote copies, remote signals or barrier semaphores. Data moves between devices by JAX's collectives and lax.ppermute only.
A program may use at most 128 MiB of HBM per device.

```python
import jax
import jax.numpy as jnp
from jax import lax

IJ = 1176
AB = 65536
EF = 8192


def raised(result, rng, source, target, parts, factor):
    owner, partner = [(jnp.arange(result.shape[position]) // (result.shape[position] // parts)).reshape([-1 if axis == position else 1 for axis in range(result.ndim)]) for position in (source, target)]
    chosen = jax.random.permutation(rng, parts)[partner]
    strong = (owner == chosen) | (owner == (partner + parts // 2) % parts)
    return jnp.where(strong, factor * result, result)


def block_scale(rng, dims, split, low, largest):
    gain, own = 1.0, jax.random.fold_in(rng, 6)
    for dim, shards_of in split:
        draws = jnp.exp(jax.random.uniform(jax.random.fold_in(own, dim), (shards_of,), jnp.float32, low / len(split), largest / len(split)))
        gain = gain * jnp.repeat(draws, dims[dim] // shards_of).reshape([-1 if axis == dim else 1 for axis in range(len(dims))])
    return gain


def normal_values(key, extent, width, bound, pieces=(), kind=jnp.bfloat16):
    level = block_scale(key, extent, pieces, -0.22, 0.18) if pieces else 1.0
    entries = jax.random.normal(key, extent, jnp.float32) * width * level
    return jnp.minimum(jnp.maximum(entries, -bound), bound).astype(kind)


def noise_with(rng, dims, width, reach, pieces, heavy, kind=jnp.bfloat16):
    values = width * jax.random.normal(rng, dims, jnp.float32)
    if pieces:
        values = values * block_scale(rng, dims, pieces, -0.22, 0.18)
    return jnp.clip(raised(values, jax.random.fold_in(rng, 3), *heavy), -reach, reach).astype(kind)


def setup_inputs(seed: int = 0) -> dict:
    keys = jax.random.split(jax.random.key(seed), 3)
    amplitudes = noise_with(keys[0], (EF, IJ), 1.0, 6.0, ((0, 256),), (0, 1, 8, 2.0), jnp.float32)
    integrals = normal_values(keys[1], (EF, AB), EF ** -0.5, 0.0625, ((0, 256),), jnp.float32)
    return {"amplitudes": amplitudes, "integrals": integrals}


def reference(amplitudes, integrals):
    contraction = lax.dot_general(amplitudes, integrals, (((0,), (0,)), ((), ())), precision=lax.Precision.HIGHEST, preferred_element_type=jnp.float32)
    return 0.5 * contraction
```

```python
import jax
import jax.numpy as jnp
from jax import lax
from jax.experimental import pallas as pl
from jax.experimental.pallas import tpu as pltpu
from jax.sharding import Mesh, PartitionSpec as P

AXES = ("x", "yh", "yl", "z", "c")
PLANE = ("x", "yh", "yl", "c")
NZ = 8
IJ, ROWS = 1176, 147
HALF = 640
CHUNKS = ((4,), (3, -3), (2, -2), (1, -1), (0,))
BIG = pltpu.CompilerParams(vmem_limit_bytes=56 * 2**20)


def pack_kernel(n, blocks_ref, *refs):
    for k in range(n):
        for c in range(2):
            for s in range(8):
                start = c * 2048 + s * 256
                refs[-1 if len(refs) == n + 1 else n + 1][
                    s, c, :, k * 256 : (k + 1) * 256
                ] = refs[k][:, start : start + 256]
    if len(refs) == n + 1:
        return
    amps_ref, out_ref, wide = refs[n:]
    wide[:, 1152:] = jnp.zeros((wide.shape[0], 128), jnp.float32)
    wide[:, :IJ] = amps_ref[...]
    for c in range(2):
        for s in range(8):
            out_ref[s, c, :, n * 256 :] = wide[:, c * HALF : (c + 1) * HALF]


def pack(integrals, blocks, n, amplitudes=None):
    rows = integrals.shape[0]
    width = n * 256 + (0 if amplitudes is None else HALF)
    specs = [
        pl.BlockSpec((rows, 4096), lambda y, b, k=k: (0, y * NZ + b[k])) for k in range(n)
    ]
    extra, scratch = [], []
    if amplitudes is not None:
        specs.append(pl.BlockSpec((rows, IJ), lambda y, b: (0, 0)))
        extra.append(amplitudes)
        scratch.append(pltpu.VMEM((rows, 2 * HALF), jnp.float32))
    out = pl.pallas_call(
        lambda *refs: pack_kernel(n, *refs),
        out_shape=jax.ShapeDtypeStruct((8, 4, rows, width), jnp.float32),
        grid_spec=pltpu.PrefetchScalarGridSpec(
            num_scalar_prefetch=1,
            grid=(2,),
            in_specs=specs,
            out_specs=pl.BlockSpec((8, 2, rows, width), lambda y, b: (0, y, 0, 0)),
            scratch_shapes=scratch,
        ),
        compiler_params=BIG,
        cost_estimate=pl.CostEstimate(
            flops=0, bytes_accessed=64 * rows * width * 4, transcendentals=0
        ),
        name="pack",
    )(blocks, *[integrals] * n, *extra)
    return out.reshape(32, rows, width)


def prepare_kernel(in_ref, high_ref, low_ref):
    value = (0.5 * in_ref[...]).T
    high = value.astype(jnp.bfloat16)
    high_ref[...] = high
    low_ref[...] = (value - high.astype(jnp.float32)).astype(jnp.bfloat16)


def prepare(slab, first):
    depth = slab.shape[0]
    half = jax.ShapeDtypeStruct((HALF, depth), jnp.bfloat16)
    spec = pl.BlockSpec((128, depth), lambda k: (k, 0))
    return pl.pallas_call(
        prepare_kernel,
        out_shape=(half, half),
        grid=(HALF // 128,),
        in_specs=[pl.BlockSpec((depth, 128), lambda k: (0, first + k))],
        out_specs=(spec, spec),
        compiler_params=BIG,
        cost_estimate=pl.CostEstimate(
            flops=0, bytes_accessed=depth * HALF * 8, transcendentals=0
        ),
        name="prepare",
    )(slab)


def product_kernel(core_ref, ha_ref, la_ref, hb_ref, lb_ref, v_ref, out_ref, vh, vl):
    piece = v_ref[...]
    high = piece.astype(jnp.bfloat16)
    vh[...] = high
    vl[...] = (piece - high.astype(jnp.float32)).astype(jnp.bfloat16)

    def dot(left_side, right_side):
        return jnp.dot(left_side, right_side, preferred_element_type=jnp.float32)

    core = core_ref[0]
    for which, h_ref, l_ref in ((core, ha_ref, la_ref), (1 - core, hb_ref, lb_ref)):
        for start in range(0, HALF, 320):
            tile = slice(start, start + 320)
            value = dot(l_ref[tile], vh[...]) + dot(h_ref[tile], vl[...])
            value += dot(h_ref[tile], vh[...])
            rows = pl.ds(pl.multiple_of(which * HALF + start, 8), 320)
            out_ref[0, rows] = value


def first_kernel(amps_ref, v_ref, out_ref):
    def split(value):
        high = value.astype(jnp.bfloat16)
        return high, (value - high.astype(jnp.float32)).astype(jnp.bfloat16)

    def dot(left_side, right_side):
        return lax.dot_general(
            left_side,
            right_side,
            (((0,), (0,)), ((), ())),
            preferred_element_type=jnp.float32,
        )

    th, tl = split(0.5 * amps_ref[...])
    vh, vl = split(v_ref[...])
    out_ref[...] = dot(tl, vh) + dot(th, vl) + dot(th, vh)


def first(amps, slab):
    depth = amps.shape[0]
    return pl.pallas_call(
        first_kernel,
        out_shape=jax.ShapeDtypeStruct((HALF, 256), jnp.float32),
        grid=(1,),
        in_specs=[
            pl.BlockSpec((depth, HALF), lambda k: (0, 0)),
            pl.BlockSpec((depth, 256), lambda k: (0, 0)),
        ],
        out_specs=pl.BlockSpec((HALF, 256), lambda k: (0, 0)),
        compiler_params=BIG,
        cost_estimate=pl.CostEstimate(
            flops=6 * HALF * depth * 256,
            bytes_accessed=4 * depth * (HALF + 256) + HALF * 1024,
            transcendentals=0,
        ),
        name="first",
    )(amps, slab)


def join_kernel(half_ref, sum_ref, product_ref, out_ref):
    low, high = slice(0, HALF), slice(HALF, IJ)
    is_low = half_ref[0] == 0

    @pl.when(is_low)
    def _():
        out_ref[low] = product_ref[0, low] + sum_ref[...]
        out_ref[high] = product_ref[0, high]

    @pl.when(jnp.logical_not(is_low))
    def _():
        out_ref[low] = product_ref[0, low]
        out_ref[high] = product_ref[0, high] + sum_ref[: IJ - HALF]


def join(half, summed, product, k):
    return pl.pallas_call(
        join_kernel,
        out_shape=jax.ShapeDtypeStruct((IJ, 256), jnp.float32),
        grid_spec=pltpu.PrefetchScalarGridSpec(
            num_scalar_prefetch=1,
            grid=(1,),
            in_specs=[
                pl.BlockSpec((HALF, 256), lambda i, h: (0, 0)),
                pl.BlockSpec((1, 2 * HALF, 256), lambda i, h: (k, 0, 0)),
            ],
            out_specs=pl.BlockSpec((IJ, 256), lambda i, h: (0, 0)),
        ),
        compiler_params=BIG,
        cost_estimate=pl.CostEstimate(
            flops=HALF * 256, bytes_accessed=HALF * 5 * 1024, transcendentals=0
        ),
        name="join",
    )(half, summed, product)


def contract(core, amps, slab, n):
    depth = slab.shape[0]
    whole = pl.BlockSpec((HALF, depth), lambda k, p: (0, 0))
    return pl.pallas_call(
        product_kernel,
        out_shape=jax.ShapeDtypeStruct((n, 2 * HALF, 256), jnp.float32),
        grid_spec=pltpu.PrefetchScalarGridSpec(
            num_scalar_prefetch=1,
            grid=(n,),
            in_specs=[whole] * 4 + [pl.BlockSpec((depth, 256), lambda k, p: (0, k))],
            out_specs=pl.BlockSpec((1, 2 * HALF, 256), lambda k, p: (k, 0, 0)),
            scratch_shapes=[pltpu.VMEM((depth, 256), jnp.bfloat16)] * 2,
        ),
        compiler_params=BIG,
        cost_estimate=pl.CostEstimate(
            flops=6 * n * 2 * HALF * depth * 256,
            bytes_accessed=8 * depth * HALF + n * (depth + 2 * HALF) * 1024,
            transcendentals=0,
        ),
        name="product",
    )(core, *amps, slab)


def on_device(amplitudes, integrals):
    rows = integrals.shape[0]
    z = lax.axis_index("z")
    core = lax.axis_index("c").astype(jnp.int32).reshape(1)
    up = [(i, (i + 1) % NZ) for i in range(NZ)]
    down = [(i, (i - 1) % NZ) for i in range(NZ)]

    def swap(sent):
        got = lax.all_to_all(sent, PLANE, split_axis=0, concat_axis=0, tiled=True)
        return got.reshape(32 * rows, -1)

    sent = []
    for place, offsets in enumerate(CHUNKS):
        blocks = ((z + jnp.array(offsets, jnp.int32) + NZ) % NZ).astype(jnp.int32)
        sent.append(pack(integrals, blocks, len(offsets), None if place else amplitudes))

    slab = swap(sent[0])
    slab, *sent[1:] = lax.optimization_barrier((slab, *sent[1:]))
    width = len(CHUNKS[0]) * 256
    own, sent[1] = lax.optimization_barrier((slab[:, width:], sent[1]))
    other = lax.ppermute(own, "c", [(0, 1), (1, 0)])
    right, left = first(own, slab), first(other, slab)
    own, other, right, left = lax.optimization_barrier((own, other, right, left))
    amps = (*prepare(own, 0), *prepare(other, 0))

    for place in range(1, 4):
        right = lax.ppermute(right, "z", up)
        left = lax.ppermute(left, "z", down)
        slab = swap(sent[place])
        if place == 1:
            right, left, slab, sent[2], *amps = lax.optimization_barrier(
                (right, left, slab, sent[2], *amps)
            )
        product = contract(core, amps, slab, 2)
        if place == 3:
            product, sent[4] = lax.optimization_barrier((product, sent[4]))
        if place == 1:
            right, left = join(core, right, product, 0), join(1 - core, left, product, 1)
        else:
            right, left = right + product[0, :IJ], left + product[1, :IJ]
    right = lax.ppermute(right, "z", up)
    left = lax.ppermute(left, "z", down)
    own = contract(core, amps, swap(sent[4]), 1)[0, :IJ]
    total = (own + right + left).reshape(8, ROWS, 256)
    got = lax.all_to_all(total, ("x", "yh"), split_axis=0, concat_axis=0, tiled=True)
    return got.transpose(1, 0, 2).reshape(ROWS, 8 * 256)


def solution(mesh):
    fine = Mesh(mesh.devices.reshape(4, 2, 2, NZ, 2), AXES)
    return jax.shard_map(
        on_device,
        mesh=fine,
        in_specs=(P(AXES, None), P(AXES, None)),
        out_specs=P(("x", "yh"), ("yl", "z", "c")),
        check_vma=False,
    )
```

```python
import jax
import jax.numpy as jnp
from jax import lax
from jax.experimental import pallas as pl
from jax.experimental.pallas import tpu as pltpu
from jax.sharding import Mesh, PartitionSpec as P

AXES = ("x", "yh", "yl", "z", "c")
PLANE = ("x", "yh", "yl", "c")
NZ = 8
IJ, ROWS = 1176, 147
HALF = 640
CHUNKS = ((4,), (3, -3), (2, -2), (1, -1), (0,))
SMALL = pltpu.CompilerParams(vmem_limit_bytes=16 * 2**20)
BIG = pltpu.CompilerParams(vmem_limit_bytes=56 * 2**20)


def pack_kernel(n, blocks_ref, *refs):
    for k in range(n):
        for c in range(2):
            for s in range(8):
                start = c * 2048 + s * 256
                refs[-1 if len(refs) == n + 1 else n + 1][
                    s, c, :, k * 256 : (k + 1) * 256
                ] = refs[k][:, start : start + 256]
    if len(refs) == n + 1:
        return
    amps_ref, out_ref, wide = refs[n:]
    wide[:, 1152:] = jnp.zeros((wide.shape[0], 128), jnp.float32)
    wide[:, :IJ] = amps_ref[...]
    for c in range(2):
        for s in range(8):
            out_ref[s, c, :, n * 256 :] = wide[:, c * HALF : (c + 1) * HALF]


def pack(integrals, blocks, n, amplitudes=None):
    rows = integrals.shape[0]
    width = n * 256 + (0 if amplitudes is None else HALF)
    specs = [
        pl.BlockSpec((rows, 4096), lambda y, b, k=k: (0, y * NZ + b[k])) for k in range(n)
    ]
    extra, scratch = [], []
    if amplitudes is not None:
        specs.append(pl.BlockSpec((rows, IJ), lambda y, b: (0, 0)))
        extra.append(amplitudes)
        scratch.append(pltpu.VMEM((rows, 2 * HALF), jnp.float32))
    out = pl.pallas_call(
        lambda *refs: pack_kernel(n, *refs),
        out_shape=jax.ShapeDtypeStruct((8, 4, rows, width), jnp.float32),
        grid_spec=pltpu.PrefetchScalarGridSpec(
            num_scalar_prefetch=1,
            grid=(2,),
            in_specs=specs,
            out_specs=pl.BlockSpec((8, 2, rows, width), lambda y, b: (0, y, 0, 0)),
            scratch_shapes=scratch,
        ),
        compiler_params=BIG,
        cost_estimate=pl.CostEstimate(
            flops=0, bytes_accessed=64 * rows * width * 4, transcendentals=0
        ),
        name="pack",
    )(blocks, *[integrals] * n, *extra)
    return out.reshape(32, rows, width)


def prepare_kernel(in_ref, high_ref, low_ref):
    value = (0.5 * in_ref[...]).T
    high = value.astype(jnp.bfloat16)
    high_ref[...] = high
    low_ref[...] = (value - high.astype(jnp.float32)).astype(jnp.bfloat16)


def prepare(slab, first):
    depth = slab.shape[0]
    half = jax.ShapeDtypeStruct((HALF, depth), jnp.bfloat16)
    spec = pl.BlockSpec((128, depth), lambda k: (k, 0))
    return pl.pallas_call(
        prepare_kernel,
        out_shape=(half, half),
        grid=(HALF // 128,),
        in_specs=[pl.BlockSpec((depth, 128), lambda k: (0, first + k))],
        out_specs=(spec, spec),
        compiler_params=SMALL,
        cost_estimate=pl.CostEstimate(
            flops=0, bytes_accessed=depth * HALF * 8, transcendentals=0
        ),
        name="prepare",
    )(slab)


def first_kernel(amps_ref, v_ref, out_ref):
    def split(value):
        high = value.astype(jnp.bfloat16)
        return high, (value - high.astype(jnp.float32)).astype(jnp.bfloat16)

    def dot(left_side, right_side):
        return lax.dot_general(
            left_side,
            right_side,
            (((0,), (0,)), ((), ())),
            preferred_element_type=jnp.float32,
        )

    th, tl = split(0.5 * amps_ref[...])
    vh, vl = split(v_ref[...])
    out_ref[...] = dot(tl, vh) + dot(th, vl) + dot(th, vh)


def first(amps, slab):
    depth = amps.shape[0]
    return pl.pallas_call(
        first_kernel,
        out_shape=jax.ShapeDtypeStruct((HALF, 256), jnp.float32),
        grid=(1,),
        in_specs=[
            pl.BlockSpec((depth, HALF), lambda k: (0, 0)),
            pl.BlockSpec((depth, 256), lambda k: (0, 0)),
        ],
        out_specs=pl.BlockSpec((HALF, 256), lambda k: (0, 0)),
        compiler_params=SMALL,
        cost_estimate=pl.CostEstimate(
            flops=6 * HALF * depth * 256,
            bytes_accessed=4 * depth * (HALF + 256) + HALF * 1024,
            transcendentals=0,
        ),
        name="first",
    )(amps, slab)


def product_kernel(n, core_ref, ha_ref, la_ref, hb_ref, lb_ref, v_ref, *refs):
    outs, sums = refs[-2 - n : -2], refs[: -2 - n]
    vh, vl = refs[-2:]
    step = pl.program_id(0)

    @pl.when(step == 0)
    def _():
        piece = v_ref[...]
        high = piece.astype(jnp.bfloat16)
        vh[...] = high
        vl[...] = (piece - high.astype(jnp.float32)).astype(jnp.bfloat16)

    def dot(left_side, right_side):
        return jnp.dot(left_side, right_side, preferred_element_type=jnp.float32)

    def rows(h_ref, l_ref, gets_sum):
        value = dot(l_ref[...], vh[...]) + dot(h_ref[...], vl[...])
        value += dot(h_ref[...], vh[...])
        for k in range(n):
            block = value[:, k * 256 : (k + 1) * 256]
            outs[k][...] = block + sums[k][...] if sums and k == gets_sum else block

    pl.when(step < 2)(lambda: rows(ha_ref, la_ref, 0))
    pl.when(step >= 2)(lambda: rows(hb_ref, lb_ref, 1))


def contract(core, amps, slab, n, sums=()):
    depth = slab.shape[0]

    def own(m):
        return jnp.minimum(m, 1)

    def other(m):
        return jnp.maximum(m - 2, 0)

    def place(m, core):
        return jnp.where(m < 2, core[0] * 2 + m, (1 - core[0]) * 2 + m - 2), 0

    return pl.pallas_call(
        lambda *refs: product_kernel(n, *refs),
        out_shape=[jax.ShapeDtypeStruct((IJ, 256), jnp.float32)] * n,
        grid_spec=pltpu.PrefetchScalarGridSpec(
            num_scalar_prefetch=1,
            grid=(4,),
            in_specs=[pl.BlockSpec((320, depth), lambda m, c: (own(m), 0))] * 2
            + [pl.BlockSpec((320, depth), lambda m, c: (other(m), 0))] * 2
            + [pl.BlockSpec((depth, n * 256), lambda m, c: (0, 0))]
            + [
                pl.BlockSpec((320, 256), lambda m, c: (own(m), 0)),
                pl.BlockSpec((320, 256), lambda m, c: (other(m), 0)),
            ][: len(sums)],
            out_specs=[pl.BlockSpec((320, 256), place)] * n,
            scratch_shapes=[pltpu.VMEM((depth, n * 256), jnp.bfloat16)] * 2,
        ),
        compiler_params=BIG,
        cost_estimate=pl.CostEstimate(
            flops=6 * n * IJ * depth * 256,
            bytes_accessed=8 * depth * HALF + n * (depth + IJ) * 1024,
            transcendentals=0,
        ),
        name="product",
    )(core, *amps, slab, *sums)


def on_device(amplitudes, integrals):
    rows = integrals.shape[0]
    z = lax.axis_index("z")
    core = lax.axis_index("c").astype(jnp.int32).reshape(1)
    up = [(i, (i + 1) % NZ) for i in range(NZ)]
    down = [(i, (i - 1) % NZ) for i in range(NZ)]

    def swap(sent):
        got = lax.all_to_all(sent, PLANE, split_axis=0, concat_axis=0, tiled=True)
        return got.reshape(32 * rows, -1)

    sent = []
    for place, offsets in enumerate(CHUNKS):
        blocks = ((z + jnp.array(offsets, jnp.int32) + NZ) % NZ).astype(jnp.int32)
        sent.append(pack(integrals, blocks, len(offsets), None if place else amplitudes))

    slab = swap(sent[0])
    slab, *sent[1:] = lax.optimization_barrier((slab, *sent[1:]))
    width = len(CHUNKS[0]) * 256
    own = slab[:, width:]
    other = lax.ppermute(own, "c", [(0, 1), (1, 0)])
    right, left = first(own, slab), first(other, slab)
    own, other, right, left = lax.optimization_barrier((own, other, right, left))
    amps = (*prepare(own, 0), *prepare(other, 0))

    for place in range(1, 4):
        right = lax.ppermute(right, "z", up)
        left = lax.ppermute(left, "z", down)
        slab = swap(sent[place])
        if place == 1:
            right, left, slab, sent[2], *amps = lax.optimization_barrier(
                (right, left, slab, sent[2], *amps)
            )
            right, left = contract(core, amps, slab, 2, (right, left))
            continue
        ups, downs = contract(core, amps, slab, 2)
        right, left = right + ups, left + downs
    right = lax.ppermute(right, "z", up)
    left = lax.ppermute(left, "z", down)
    own = contract(core, amps, swap(sent[4]), 1)[0]
    total = (own + right + left).reshape(8, ROWS, 256)
    got = lax.all_to_all(total, ("x", "yh"), split_axis=0, concat_axis=0, tiled=True)
    return got.transpose(1, 0, 2).reshape(ROWS, 8 * 256)


def solution(mesh):
    fine = Mesh(mesh.devices.reshape(4, 2, 2, NZ, 2), AXES)
    return jax.shard_map(
        on_device,
        mesh=fine,
        in_specs=(P(AXES, None), P(AXES, None)),
        out_specs=P(("x", "yh"), ("yl", "z", "c")),
        check_vma=False,
    )
```

```python
import jax
import jax.numpy as jnp
from jax import lax
from jax.experimental import pallas as pl
from jax.experimental.pallas import tpu as pltpu
from jax.sharding import Mesh, PartitionSpec as P

AXES = ("x", "yh", "yl", "z", "c")
PLANE = ("x", "yh", "yl", "c")
NZ = 8
IJ, ROWS = 1176, 147
HALF = 640
CHUNKS = ((4,), (3, -3), (2, -2), (1, -1), (0,))
SMALL = pltpu.CompilerParams(vmem_limit_bytes=16 * 2**20)
BIG = pltpu.CompilerParams(vmem_limit_bytes=56 * 2**20)


def pack_kernel(n, blocks_ref, *refs):
    for k in range(n):
        for c in range(2):
            for s in range(8):
                start = c * 2048 + s * 256
                refs[-1 if len(refs) == n + 1 else n + 1][
                    s, c, :, k * 256 : (k + 1) * 256
                ] = refs[k][:, start : start + 256]
    if len(refs) == n + 1:
        return
    amps_ref, out_ref, wide = refs[n:]
    wide[:, 1152:] = jnp.zeros((wide.shape[0], 128), jnp.float32)
    wide[:, :IJ] = amps_ref[...]
    for c in range(2):
        for s in range(8):
            out_ref[s, c, :, n * 256 :] = wide[:, c * HALF : (c + 1) * HALF]


def pack(integrals, blocks, n, amplitudes=None):
    rows = integrals.shape[0]
    width = n * 256 + (0 if amplitudes is None else HALF)
    specs = [
        pl.BlockSpec((rows, 4096), lambda y, b, k=k: (0, y * NZ + b[k])) for k in range(n)
    ]
    extra, scratch = [], []
    if amplitudes is not None:
        specs.append(pl.BlockSpec((rows, IJ), lambda y, b: (0, 0)))
        extra.append(amplitudes)
        scratch.append(pltpu.VMEM((rows, 2 * HALF), jnp.float32))
    out = pl.pallas_call(
        lambda *refs: pack_kernel(n, *refs),
        out_shape=jax.ShapeDtypeStruct((8, 4, rows, width), jnp.float32),
        grid_spec=pltpu.PrefetchScalarGridSpec(
            num_scalar_prefetch=1,
            grid=(2,),
            in_specs=specs,
            out_specs=pl.BlockSpec((8, 2, rows, width), lambda y, b: (0, y, 0, 0)),
            scratch_shapes=scratch,
        ),
        compiler_params=BIG,
        cost_estimate=pl.CostEstimate(
            flops=0, bytes_accessed=64 * rows * width * 4, transcendentals=0
        ),
        name="pack",
    )(blocks, *[integrals] * n, *extra)
    return out.reshape(32, rows, width)


def first_kernel(amps_ref, v_ref, out_ref):
    def split(value):
        high = value.astype(jnp.bfloat16)
        return high, (value - high.astype(jnp.float32)).astype(jnp.bfloat16)

    def dot(left_side, right_side):
        return lax.dot_general(
            left_side,
            right_side,
            (((0,), (0,)), ((), ())),
            preferred_element_type=jnp.float32,
        )

    th, tl = split(0.5 * amps_ref[...])
    vh, vl = split(v_ref[...])
    out_ref[...] = dot(tl, vh) + dot(th, vl) + dot(th, vh)


def first(amps, slab):
    depth = amps.shape[0]
    return pl.pallas_call(
        first_kernel,
        out_shape=jax.ShapeDtypeStruct((HALF, 256), jnp.float32),
        grid=(1,),
        in_specs=[
            pl.BlockSpec((depth, HALF), lambda k: (0, 0)),
            pl.BlockSpec((depth, 256), lambda k: (0, 0)),
        ],
        out_specs=pl.BlockSpec((HALF, 256), lambda k: (0, 0)),
        compiler_params=SMALL,
        cost_estimate=pl.CostEstimate(
            flops=6 * HALF * depth * 256,
            bytes_accessed=4 * depth * (HALF + 256) + HALF * 1024,
            transcendentals=0,
        ),
        name="first",
    )(amps, slab)


def contract(left_side, right_side):
    return lax.dot_general(
        left_side,
        right_side,
        (((0,), (0,)), ((), ())),
        precision=lax.Precision.HIGH,
        preferred_element_type=jnp.float32,
    )


def on_device(amplitudes, integrals):
    rows = integrals.shape[0]
    z = lax.axis_index("z")
    core = lax.axis_index("c").astype(jnp.int32).reshape(1)
    up = [(i, (i + 1) % NZ) for i in range(NZ)]
    down = [(i, (i - 1) % NZ) for i in range(NZ)]

    def swap(sent):
        got = lax.all_to_all(sent, PLANE, split_axis=0, concat_axis=0, tiled=True)
        return got.reshape(32 * rows, -1)

    sent = []
    for place, offsets in enumerate(CHUNKS):
        blocks = ((z + jnp.array(offsets, jnp.int32) + NZ) % NZ).astype(jnp.int32)
        sent.append(pack(integrals, blocks, len(offsets), None if place else amplitudes))

    slab = swap(sent[0])
    slab, *sent[1:] = lax.optimization_barrier((slab, *sent[1:]))
    width = len(CHUNKS[0]) * 256
    own = slab[:, width:]
    other = lax.ppermute(own, "c", [(0, 1), (1, 0)])
    is_first = core[0] == 0

    def in_order(one, two, axis):
        return (
            jnp.where(is_first, one, two),
            lax.slice_in_dim(jnp.where(is_first, two, one), 0, IJ - HALF, axis=axis),
        )

    right, left = in_order(first(own, slab), first(other, slab), 0)
    own, other, right, left = lax.optimization_barrier((own, other, right, left))
    amps = 0.5 * jnp.concatenate(in_order(own, other, 1), axis=1)

    for place in range(1, 4):
        right = lax.ppermute(right, "z", up)
        left = lax.ppermute(left, "z", down)
        slab = swap(sent[place])
        if place == 1:
            right, left, slab, amps = lax.optimization_barrier((right, left, slab, amps))
            right = jnp.pad(right, ((0, IJ - HALF), (0, 0)))
            left = jnp.pad(left, ((HALF, 0), (0, 0)))
        product = lax.optimization_barrier(contract(amps, slab))
        right, left = right + product[:, :256], left + product[:, 256:]
    right = lax.ppermute(right, "z", up)
    left = lax.ppermute(left, "z", down)
    total = (contract(amps, swap(sent[4])) + right + left).reshape(8, ROWS, 256)
    got = lax.all_to_all(total, ("x", "yh"), split_axis=0, concat_axis=0, tiled=True)
    return got.transpose(1, 0, 2).reshape(ROWS, 8 * 256)


def solution(mesh):
    fine = Mesh(mesh.devices.reshape(4, 2, 2, NZ, 2), AXES)
    return jax.shard_map(
        on_device,
        mesh=fine,
        in_specs=(P(AXES, None), P(AXES, None)),
        out_specs=P(("x", "yh"), ("yl", "z", "c")),
        check_vma=False,
    )
```

```python
import jax
import jax.numpy as jnp
from jax import lax
from jax.experimental import pallas as pl
from jax.experimental.pallas import tpu as pltpu
from jax.sharding import Mesh, PartitionSpec as P

AXES = ("x", "yh", "yl", "z", "c")
PLANE = ("x", "yh", "yl", "c")
NZ = 8
IJ, ROWS = 1176, 147
HALF = 640
CHUNKS = ((4,), (3, -3), (2, -2), (1, -1), (0,))
SMALL = pltpu.CompilerParams(vmem_limit_bytes=16 * 2**20)
BIG = pltpu.CompilerParams(vmem_limit_bytes=56 * 2**20)


def pack_kernel(n, blocks_ref, *refs):
    for k in range(n):
        for c in range(2):
            for s in range(8):
                start = c * 2048 + s * 256
                refs[-1 if len(refs) == n + 1 else n + 1][
                    s, c, :, k * 256 : (k + 1) * 256
                ] = refs[k][:, start : start + 256]
    if len(refs) == n + 1:
        return
    amps_ref, out_ref, wide = refs[n:]
    wide[:, 1152:] = jnp.zeros((wide.shape[0], 128), jnp.float32)
    wide[:, :IJ] = amps_ref[...]
    for c in range(2):
        for s in range(8):
            out_ref[s, c, :, n * 256 :] = wide[:, c * HALF : (c + 1) * HALF]


def pack(integrals, blocks, n, amplitudes=None):
    rows = integrals.shape[0]
    width = n * 256 + (0 if amplitudes is None else HALF)
    specs = [
        pl.BlockSpec((rows, 4096), lambda y, b, k=k: (0, y * NZ + b[k])) for k in range(n)
    ]
    extra, scratch = [], []
    if amplitudes is not None:
        specs.append(pl.BlockSpec((rows, IJ), lambda y, b: (0, 0)))
        extra.append(amplitudes)
        scratch.append(pltpu.VMEM((rows, 2 * HALF), jnp.float32))
    out = pl.pallas_call(
        lambda *refs: pack_kernel(n, *refs),
        out_shape=jax.ShapeDtypeStruct((8, 4, rows, width), jnp.float32),
        grid_spec=pltpu.PrefetchScalarGridSpec(
            num_scalar_prefetch=1,
            grid=(2,),
            in_specs=specs,
            out_specs=pl.BlockSpec((8, 2, rows, width), lambda y, b: (0, y, 0, 0)),
            scratch_shapes=scratch,
        ),
        compiler_params=BIG,
        cost_estimate=pl.CostEstimate(
            flops=0, bytes_accessed=64 * rows * width * 4, transcendentals=0
        ),
        name="pack",
    )(blocks, *[integrals] * n, *extra)
    return out.reshape(32, rows, width)


def first_kernel(amps_ref, v_ref, out_ref):
    def split(value):
        high = value.astype(jnp.bfloat16)
        return high, (value - high.astype(jnp.float32)).astype(jnp.bfloat16)

    def dot(left_side, right_side):
        return lax.dot_general(
            left_side,
            right_side,
            (((0,), (0,)), ((), ())),
            preferred_element_type=jnp.float32,
        )

    th, tl = split(0.5 * amps_ref[...])
    vh, vl = split(v_ref[...])
    out_ref[...] = dot(tl, vh) + dot(th, vl) + dot(th, vh)


def first(amps, slab):
    depth = amps.shape[0]
    return pl.pallas_call(
        first_kernel,
        out_shape=jax.ShapeDtypeStruct((HALF, 256), jnp.float32),
        grid=(1,),
        in_specs=[
            pl.BlockSpec((depth, HALF), lambda k: (0, 0)),
            pl.BlockSpec((depth, 256), lambda k: (0, 0)),
        ],
        out_specs=pl.BlockSpec((HALF, 256), lambda k: (0, 0)),
        compiler_params=SMALL,
        cost_estimate=pl.CostEstimate(
            flops=6 * HALF * depth * 256,
            bytes_accessed=4 * depth * (HALF + 256) + HALF * 1024,
            transcendentals=0,
        ),
        name="first",
    )(amps, slab)


def contract(left_side, right_side):
    return lax.dot_general(
        left_side,
        right_side,
        (((0,), (0,)), ((), ())),
        precision=lax.Precision.HIGH,
        preferred_element_type=jnp.float32,
    )


def on_device(amplitudes, integrals):
    rows = integrals.shape[0]
    z = lax.axis_index("z")
    core = lax.axis_index("c").astype(jnp.int32).reshape(1)
    up = [(i, (i + 1) % NZ) for i in range(NZ)]
    down = [(i, (i - 1) % NZ) for i in range(NZ)]

    def swap(sent):
        got = lax.all_to_all(sent, PLANE, split_axis=0, concat_axis=0, tiled=True)
        return got.reshape(32 * rows, -1)

    sent = []
    for place, offsets in enumerate(CHUNKS):
        blocks = ((z + jnp.array(offsets, jnp.int32) + NZ) % NZ).astype(jnp.int32)
        sent.append(pack(integrals, blocks, len(offsets), None if place else amplitudes))

    slab = swap(sent[0])
    slab, *sent[1:] = lax.optimization_barrier((slab, *sent[1:]))
    width = len(CHUNKS[0]) * 256
    own = slab[:, width:]
    other = lax.ppermute(own, "c", [(0, 1), (1, 0)])
    is_first = core[0] == 0

    def in_order(one, two, axis):
        return (
            jnp.where(is_first, one, two),
            lax.slice_in_dim(jnp.where(is_first, two, one), 0, IJ - HALF, axis=axis),
        )

    right, left = in_order(first(own, slab), first(other, slab), 0)
    own, other, right, left = lax.optimization_barrier((own, other, right, left))
    amps = 0.5 * jnp.concatenate(in_order(own, other, 1), axis=1)
    amps, sent[2] = lax.optimization_barrier((amps, sent[2]))

    for place in range(1, 4):
        right = lax.ppermute(right, "z", up)
        left = lax.ppermute(left, "z", down)
        slab = swap(sent[place])
        if place == 1:
            right, left, slab, amps = lax.optimization_barrier((right, left, slab, amps))
            right = jnp.pad(right, ((0, IJ - HALF), (0, 0)))
            left = jnp.pad(left, ((HALF, 0), (0, 0)))
        product = lax.optimization_barrier(contract(amps, slab))
        right, left = right + product[:, :256], left + product[:, 256:]
    right = lax.ppermute(right, "z", up)
    left = lax.ppermute(left, "z", down)
    total = (contract(amps, swap(sent[4])) + right + left).reshape(8, ROWS, 256)
    got = lax.all_to_all(total, ("x", "yh"), split_axis=0, concat_axis=0, tiled=True)
    return got.transpose(1, 0, 2).reshape(ROWS, 8 * 256)


def solution(mesh):
    fine = Mesh(mesh.devices.reshape(4, 2, 2, NZ, 2), AXES)
    return jax.shard_map(
        on_device,
        mesh=fine,
        in_specs=(P(AXES, None), P(AXES, None)),
        out_specs=P(("x", "yh"), ("yl", "z", "c")),
        check_vma=False,
    )
```

```python
import jax
import jax.numpy as jnp
from jax import lax
from jax.experimental import pallas as pl
from jax.experimental.pallas import tpu as pltpu
from jax.sharding import Mesh, PartitionSpec as P

AXES = ("x", "yh", "yl", "z", "c")
PLANE = ("x", "yh", "yl", "c")
NZ = 8
IJ, ROWS = 1176, 147
HALF = 640
CHUNKS = ((4,), (3, -3), (2, -2), (1, -1), (0,))
SMALL = pltpu.CompilerParams(vmem_limit_bytes=16 * 2**20)
BIG = pltpu.CompilerParams(vmem_limit_bytes=56 * 2**20)


def pack_kernel(n, blocks_ref, *refs):
    out_ref = refs[n] if len(refs) == n + 1 else refs[n + 1]
    for k in range(n):
        for s in range(8):
            piece = refs[k][:, s * 256 : (s + 1) * 256]
            out_ref[s, 0, :, k * 256 : (k + 1) * 256] = piece
    if len(refs) == n + 1:
        return
    amps_ref, wide = refs[n], refs[n + 2]
    wide[:, 1152:] = jnp.zeros((wide.shape[0], 128), jnp.float32)
    wide[:, :IJ] = amps_ref[...]
    for c in range(2):

        @pl.when(pl.program_id(1) == c)
        def _(c=c):
            for s in range(8):
                out_ref[s, 0, :, n * 256 :] = wide[:, c * HALF : (c + 1) * HALF]


def pack(integrals, blocks, n, amplitudes=None):
    rows = integrals.shape[0]
    width = n * 256 + (0 if amplitudes is None else HALF)
    specs = [
        pl.BlockSpec((rows, 2048), lambda y, c, b, k=k: (0, (y * NZ + b[k]) * 2 + c))
        for k in range(n)
    ]
    extra, scratch = [], []
    if amplitudes is not None:
        specs.append(pl.BlockSpec((rows, IJ), lambda y, c, b: (0, 0)))
        extra.append(amplitudes)
        scratch.append(pltpu.VMEM((rows, 2 * HALF), jnp.float32))
    out = pl.pallas_call(
        lambda *refs: pack_kernel(n, *refs),
        out_shape=jax.ShapeDtypeStruct((8, 4, rows, width), jnp.float32),
        grid_spec=pltpu.PrefetchScalarGridSpec(
            num_scalar_prefetch=1,
            grid=(2, 2),
            in_specs=specs,
            out_specs=pl.BlockSpec((8, 1, rows, width), lambda y, c, b: (0, y * 2 + c, 0, 0)),
            scratch_shapes=scratch,
        ),
        compiler_params=BIG,
        cost_estimate=pl.CostEstimate(
            flops=0, bytes_accessed=64 * rows * width * 4, transcendentals=0
        ),
        name="pack",
    )(blocks, *[integrals] * n, *extra)
    return out.reshape(32, rows, width)


def first_kernel(amps_ref, v_ref, out_ref):
    def split(value):
        high = value.astype(jnp.bfloat16)
        return high, (value - high.astype(jnp.float32)).astype(jnp.bfloat16)

    def dot(left_side, right_side):
        return lax.dot_general(
            left_side,
            right_side,
            (((0,), (0,)), ((), ())),
            preferred_element_type=jnp.float32,
        )

    th, tl = split(0.5 * amps_ref[...])
    vh, vl = split(v_ref[...])
    out_ref[...] = dot(tl, vh) + dot(th, vl) + dot(th, vh)


def first(amps, slab):
    depth = amps.shape[0]
    return pl.pallas_call(
        first_kernel,
        out_shape=jax.ShapeDtypeStruct((HALF, 256), jnp.float32),
        grid=(1,),
        in_specs=[
            pl.BlockSpec((depth, HALF), lambda k: (0, 0)),
            pl.BlockSpec((depth, 256), lambda k: (0, 0)),
        ],
        out_specs=pl.BlockSpec((HALF, 256), lambda k: (0, 0)),
        compiler_params=SMALL,
        cost_estimate=pl.CostEstimate(
            flops=6 * HALF * depth * 256,
            bytes_accessed=4 * depth * (HALF + 256) + HALF * 1024,
            transcendentals=0,
        ),
        name="first",
    )(amps, slab)


def contract(left_side, right_side):
    return lax.dot_general(
        left_side,
        right_side,
        (((0,), (0,)), ((), ())),
        precision=lax.Precision.HIGH,
        preferred_element_type=jnp.float32,
    )


def on_device(amplitudes, integrals):
    rows = integrals.shape[0]
    z = lax.axis_index("z")
    core = lax.axis_index("c").astype(jnp.int32).reshape(1)
    up = [(i, (i + 1) % NZ) for i in range(NZ)]
    down = [(i, (i - 1) % NZ) for i in range(NZ)]

    def swap(sent):
        got = lax.all_to_all(sent, PLANE, split_axis=0, concat_axis=0, tiled=True)
        return got.reshape(32 * rows, -1)

    sent = []
    for place, offsets in enumerate(CHUNKS):
        blocks = ((z + jnp.array(offsets, jnp.int32) + NZ) % NZ).astype(jnp.int32)
        sent.append(pack(integrals, blocks, len(offsets), None if place else amplitudes))

    slab = swap(sent[0])
    slab, *sent[1:] = lax.optimization_barrier((slab, *sent[1:]))
    width = len(CHUNKS[0]) * 256
    own = slab[:, width:]
    other = lax.ppermute(own, "c", [(0, 1), (1, 0)])
    is_first = core[0] == 0

    def in_order(one, two, axis):
        return (
            jnp.where(is_first, one, two),
            lax.slice_in_dim(jnp.where(is_first, two, one), 0, IJ - HALF, axis=axis),
        )

    right, left = in_order(first(own, slab), first(other, slab), 0)
    own, other, right, left = lax.optimization_barrier((own, other, right, left))
    amps = 0.5 * jnp.concatenate(in_order(own, other, 1), axis=1)
    amps, sent[2] = lax.optimization_barrier((amps, sent[2]))

    for place in range(1, 4):
        right = lax.ppermute(right, "z", up)
        left = lax.ppermute(left, "z", down)
        slab = swap(sent[place])
        if place == 1:
            right, left, slab, amps = lax.optimization_barrier((right, left, slab, amps))
            right = jnp.pad(right, ((0, IJ - HALF), (0, 0)))
            left = jnp.pad(left, ((HALF, 0), (0, 0)))
        product = lax.optimization_barrier(contract(amps, slab))
        right, left = right + product[:, :256], left + product[:, 256:]
    right = lax.ppermute(right, "z", up)
    left = lax.ppermute(left, "z", down)
    product = lax.optimization_barrier(contract(amps, swap(sent[4])))
    total = (product + right + left).reshape(8, ROWS, 256)
    got = lax.all_to_all(total, ("x", "yh"), split_axis=0, concat_axis=0, tiled=True)
    return got.transpose(1, 0, 2).reshape(ROWS, 8 * 256)


def solution(mesh):
    fine = Mesh(mesh.devices.reshape(4, 2, 2, NZ, 2), AXES)
    return jax.shard_map(
        on_device,
        mesh=fine,
        in_specs=(P(AXES, None), P(AXES, None)),
        out_specs=P(("x", "yh"), ("yl", "z", "c")),
        check_vma=False,
    )
```
